128 devices in a mesh: mem: 4 (over y), patch: 32 (over x, z, core).
Axes of the slice: x: 4, y: 4, z: 4, core: 2. Of those that a mesh axis runs over, the one named last changes fastest.
Arguments:
- prior_states: bfloat16 [256, 524288], P('mem', 'patch'), may hold values from -6 to 6
- member_obs_images: bfloat16 [1048576, 256], P(('mem', 'patch')), may hold values from -64 to 64
- obs_residual: float32 [1048576], P(('mem', 'patch')), may hold values from -6 to 6
- obs_precision_weights: float32 [1048576], P(('mem', 'patch')), may hold values from 0.3 to 3
- region_obs_groups: int32 [512, 32], replicated, may hold values from 0 to 8191, as said below
- active_profile_tally: int32 [512], replicated, may hold values from 1 to 8
Outputs:
- analysis: bfloat16 [256, 524288], P('mem', 'patch')
The draws below stay inside these ranges and needn't reach their ends.
Inputs may be any that keep to these rules, and one draw needn't show every extreme that they name: `region_obs_groups`: in each aligned group of 4 rows (the patches of one device after relayout), every range of 64 consecutive block numbers (the observations of one device) is named by no entry or by exactly 2 entries, and exactly half of the ranges are named.
All inputs are finite; a program needn't handle non-finite values.
Results may differ from the reference program's by a relative error of at most 0.0082.
Values may be sent and summed in bfloat16 or wider, within the bound.
No kernel may reach another device: no remote copies, remote signals or barrier semaphores. Data moves between devices by JAX's collectives and lax.ppermute only.
A program may use at most 128 MiB of HBM per device.

```python
import math
import jax
import jax.numpy as jnp
from jax import lax

MEMBER_NUMBER = 256
NV = 128
CPP = 8
PATCH_DEV = 4
NB_DEV = 64
BLK = 128
CAP = 2
ITERS = 10
LB = 32
NPATCH = 512
STATE_LENGTH = 524288
NOBS = 1048576
DEVICES = 128


def draw_region_obs_groups(key, part):
    key = jax.random.fold_in(key, 11)
    entries = PATCH_DEV * LB
    named = entries // CAP
    key_src, key_blk, key_order = jax.random.split(key, 3)
    sources = jax.vmap(lambda k: jax.random.permutation(k, DEVICES)[:named])(jax.random.split(key_src, DEVICES))
    sources = jnp.repeat(sources, CAP, axis=1)
    within = jax.random.randint(key_blk, (DEVICES, entries), 0, NB_DEV)
    blocks = sources * NB_DEV + within
    orders = jax.vmap(lambda k: jax.random.permutation(k, entries))(jax.random.split(key_order, DEVICES))
    blocks = jnp.take_along_axis(blocks, orders, axis=1)
    return blocks.reshape(DEVICES * PATCH_DEV, LB).astype(jnp.int32)


def draw_member_obs_images(key, part):
    key = jax.random.fold_in(key, 23)
    pattern_total = 16
    mix_uses = 8
    list_rows = LB * BLK
    key_noise, key_pattern, key_amp, key_block, key_mass, key_pick, key_coef = jax.random.split(key, 7)
    spread = 0.15
    noise = jax.random.truncated_normal(key_noise, -4.0, 4.0, (NOBS, MEMBER_NUMBER), jnp.float32)
    amps = jax.random.truncated_normal(key_amp, -3.0, 3.0, (NOBS, pattern_total), jnp.float32)
    coefs = jax.random.truncated_normal(key_coef, -3.0, 3.0, (NOBS, mix_uses), jnp.float32)
    top_level = 3000.0
    mass_top = 800.0
    patterns = jax.random.truncated_normal(key_pattern, -3.0, 3.0, (pattern_total, MEMBER_NUMBER), jnp.float32)
    mass_patterns = jax.random.truncated_normal(key_mass, -3.0, 3.0, (MEMBER_NUMBER, MEMBER_NUMBER), jnp.float32)
    mass_levels = mass_top * jnp.exp(jnp.arange(MEMBER_NUMBER, dtype=jnp.float32) * (math.log(0.001) / (MEMBER_NUMBER - 1.0)))
    picks = jax.random.randint(key_pick, (NOBS, mix_uses), 0, MEMBER_NUMBER)
    strength = jnp.exp(jax.random.uniform(key_block, (NOBS // BLK, 1), jnp.float32, math.log(0.5), math.log(2.0)))
    strength = jnp.repeat(strength, BLK, axis=0)
    total = spread * noise
    for index in range(pattern_total):
        level = 2.0 * (top_level / 2.0) ** (index / (pattern_total - 1.0))
        factor = math.sqrt(level / list_rows)
        total = total + strength * (factor * amps[:, index:index + 1]) * patterns[index][None, :]
    mass_scale = MEMBER_NUMBER / (mix_uses * list_rows)
    for use in range(mix_uses):
        chosen = picks[:, use]
        factor = jnp.sqrt(mass_levels[chosen] * mass_scale)
        total = total + strength * (factor * coefs[:, use])[:, None] * mass_patterns[chosen]
    return jnp.clip(total, -64.0, 64.0).astype(jnp.bfloat16)


def place_ends(result, own_key, least, largest):
    spot = [jax.random.randint(jax.random.fold_in(own_key, axis), (), 0, length) for axis, length in enumerate(result.shape)]
    longest = result.shape.index(max(result.shape))
    neighbour = spot[:longest] + [(spot[longest] + 1) % result.shape[longest]] + spot[longest + 1:]
    return result.at[tuple(spot)].set(least).at[tuple(neighbour)].set(largest)


def shard_levels(stream_key, dims, pieces, smallest, largest):
    factor_of, own = 1.0, jax.random.fold_in(stream_key, 6)
    for position, blocks in pieces:
        heights = jnp.exp(jax.random.uniform(jax.random.fold_in(own, position), (blocks,), jnp.float32, smallest / len(pieces), largest / len(pieces)))
        factor_of = factor_of * jnp.repeat(heights, dims[position] // blocks).reshape([-1 if axis == position else 1 for axis in range(len(dims))])
    return factor_of


def gaussian(key, dims, width, bound, cuts=(), held_as=jnp.bfloat16):
    drawn = jax.random.normal(key, dims, jnp.float32) * width
    if len(cuts) > 0:
        drawn = shard_levels(key, dims, cuts, -0.22, 0.18) * drawn
    return jnp.clip(drawn, min=-bound, max=bound).astype(held_as)


def setup_inputs(seed: int = 0) -> dict:
    arg_keys = jax.random.split(jax.random.key(seed), 7)
    return {
        "prior_states": gaussian(arg_keys[0], (MEMBER_NUMBER, STATE_LENGTH), 1.0, 6.0, ((0, 4), (1, 32))),
        "member_obs_images": draw_member_obs_images(jax.random.fold_in(arg_keys[6], 71), 0),
        "obs_residual": gaussian(arg_keys[2], (NOBS,), 1.0, 6.0, ((0, 128),), jnp.float32),
        "obs_precision_weights": jnp.clip(jnp.exp(math.log(3.0) - 2.3025851 * jax.random.uniform(arg_keys[3], (NOBS,), jnp.float32) ** shard_levels(arg_keys[3], (NOBS,), ((0, 128),), -0.2, 0.2)), 0.3, 3.0),
        "region_obs_groups": draw_region_obs_groups(jax.random.fold_in(arg_keys[6], 71), 0),
        "active_profile_tally": place_ends(jax.random.randint(arg_keys[5], (NPATCH,), 1, CPP + 1), jax.random.fold_in(arg_keys[5], 1), 1, CPP).astype(jnp.int32),
    }


def letkf_weights(gram, ybar):
    eye = jnp.eye(MEMBER_NUMBER, dtype=jnp.float32)
    amat = (MEMBER_NUMBER - 1.0) * eye + gram
    norm = jnp.sqrt(jnp.sum(amat * amat) + 1e-06)
    ysweep = amat / norm
    zsweep = eye
    for sweep in range(ITERS):
        mid = 1.5 * eye - 0.5 * jnp.dot(zsweep, ysweep, precision=lax.Precision.HIGHEST)
        ysweep = jnp.dot(ysweep, mid, precision=lax.Precision.HIGHEST)
        zsweep = jnp.dot(mid, zsweep, precision=lax.Precision.HIGHEST)
    root_inv = zsweep / jnp.sqrt(norm)
    inner = jnp.dot(root_inv, ybar, precision=lax.Precision.HIGHEST)
    mean_w = jnp.dot(root_inv, inner, precision=lax.Precision.HIGHEST)
    return (math.sqrt(MEMBER_NUMBER - 1.0) * root_inv + mean_w[:, None]).astype(jnp.bfloat16)

def reference(prior_states, member_obs_images, obs_residual, obs_precision_weights, region_obs_groups, active_profile_tally):
    obs_mean = lax.optimization_barrier(jnp.mean(member_obs_images.astype(jnp.float32), axis=1, keepdims=True))
    root_r = jnp.sqrt(obs_precision_weights)
    weighted = ((member_obs_images.astype(jnp.float32) - obs_mean) * root_r[:, None]).astype(jnp.bfloat16)
    scaled = root_r * obs_residual
    row_blocks = weighted.reshape(-1, BLK, MEMBER_NUMBER)
    innov_blocks = scaled.reshape(-1, BLK)
    prior_average = lax.optimization_barrier(jnp.mean(prior_states.astype(jnp.float32), axis=0))
    prior_anomaly = (prior_states.astype(jnp.float32) - prior_average[None, :]).astype(jnp.bfloat16)
    vertical_extent = CPP * NV
    column = jnp.arange(vertical_extent) // NV

    def one_patch(index):
        rows = row_blocks[region_obs_groups[index]].reshape(LB * BLK, MEMBER_NUMBER)
        values = innov_blocks[region_obs_groups[index]].reshape(LB * BLK)
        gram = jnp.dot(rows.T, rows, preferred_element_type=jnp.float32)
        ybar = jnp.dot(values, rows.astype(jnp.float32), precision=lax.Precision.HIGHEST)
        weights = letkf_weights(gram, ybar)
        vertical_offset = (index * vertical_extent).astype(jnp.int32)
        nearby_anomaly = lax.dynamic_slice_in_dim(prior_anomaly, vertical_offset, vertical_extent, 1)
        nearby_average = lax.dynamic_slice_in_dim(prior_average, vertical_offset, vertical_extent, 0)
        region_prior = lax.dynamic_slice_in_dim(prior_states, vertical_offset, vertical_extent, 1).astype(jnp.float32)
        blended_states = nearby_average[None, :] + jnp.dot(weights.T, nearby_anomaly, preferred_element_type=jnp.float32)
        retain_mask = column < active_profile_tally[index]
        return jnp.where(retain_mask[None, :], blended_states, region_prior).astype(jnp.bfloat16)
    patches = lax.map(one_patch, jnp.arange(NPATCH, dtype=jnp.int32))
    return jnp.transpose(patches, (1, 0, 2)).reshape(MEMBER_NUMBER, STATE_LENGTH)
```

```python
import math

import jax
import jax.numpy as jnp
from jax import lax
from jax.experimental import pallas as pl
from jax.experimental.pallas import tpu as pltpu
from jax.sharding import PartitionSpec as P

NV = 128
BLK = 128
CAP = 2
ITERS = 10
TAIL = 16
CHUNK = 8

NT = (((1,), (1,)), ((), ()))
NN = (((1,), (0,)), ((), ()))


def dot(a, b, dims=NN):
    return lax.dot_general(a, b, dims, preferred_element_type=jnp.float32)


def iotas(shape):
    return lax.broadcasted_iota(jnp.int32, shape, 0), lax.broadcasted_iota(jnp.int32, shape, 1)


def send_kernel(
    lists_ref, img_ref, prec_ref, resid_ref, send_ref, table_ref,
    wt, innov, tail, centre, keys, keys_s, key_sem, tail_sem, sems,
):
    nmem = lax.axis_size("mem")
    npat = lax.axis_size("patch")
    groups, entries = lists_ref.shape
    members = img_ref.shape[1]
    nb_dev = wt.shape[0]
    step = pl.program_id(0)
    me_m = lax.axis_index("mem")
    me_p = lax.axis_index("patch")
    source = me_m * npat + me_p

    @pl.when(step == 0)
    def _():
        row, col = iotas((members, members))
        centre[...] = (
            jnp.where(row == col, 1.0, 0.0) - 1.0 / members
        ).astype(jnp.bfloat16)
        by_entry = lists_ref[...].T
        position, _ = iotas((entries, groups))
        mine = by_entry // nb_dev == source
        key = position * nb_dev + by_entry - source * nb_dev
        first = jnp.min(jnp.where(mine, key, entries * nb_dev), axis=0, keepdims=True)
        last = jnp.max(jnp.where(mine, key, -1), axis=0, keepdims=True)
        valid = last >= 0
        keys[0:1, :] = jnp.where(valid, first % nb_dev, -1)
        keys[1:2, :] = jnp.where(valid, last % nb_dev, -1)
        pltpu.make_async_copy(keys, keys_s, key_sem).start()
        my_row = jnp.broadcast_to(
            lists_ref[pl.ds(me_p * nmem + me_m, 1), :], (entries, entries)
        ) // nb_dev
        my_col = my_row.T
        row, col = iotas((entries, entries))
        earlier = jnp.where((my_row == my_col) & (row < col), 1, 0)
        slot = jnp.max(earlier, axis=0, keepdims=True)
        table_ref[...] = jnp.broadcast_to(my_row[0:1, :] * CAP + slot, table_ref.shape)

    root = jnp.sqrt(prec_ref[...])
    innov[pl.ds(pl.multiple_of(step * CHUNK, CHUNK), CHUNK), :] = root * resid_ref[...]
    for j in range(CHUNK):
        centred = dot(centre[...], img_ref[j * BLK : (j + 1) * BLK, :], NT)
        wt[step * CHUNK + j] = (centred * root[j : j + 1, :]).astype(jnp.bfloat16)

    @pl.when(step == pl.num_programs(0) - 1)
    def _():
        pltpu.make_async_copy(keys, keys_s, key_sem).wait()
        row, _ = iotas((TAIL, BLK))

        def copies(g):
            dest = (g % nmem) * npat + g // nmem
            return [
                pltpu.make_async_copy(
                    wt.at[jnp.maximum(keys_s[c, g], 0)],
                    send_ref.at[dest, pl.ds(c * members, members), :],
                    sems.at[c, g],
                )
                for c in range(CAP)
            ]

        def start(g, _):
            @pl.when(keys_s[0, g] >= 0)
            def _():
                for copy in copies(g):
                    copy.start()

            return 0

        lax.fori_loop(0, groups, start, 0)

        def fill(g, _):
            dest = (g % nmem) * npat + g // nmem
            one = innov[pl.ds(jnp.maximum(keys_s[0, g], 0), 1), :]
            two = innov[pl.ds(jnp.maximum(keys_s[1, g], 0), 1), :]
            tail[dest] = jnp.where(row == 0, one, jnp.where(row == 1, two, 0.0)).astype(jnp.bfloat16)
            return 0

        lax.fori_loop(0, groups, fill, 0)
        tails = pltpu.make_async_copy(
            tail, send_ref.at[:, pl.ds(CAP * members, TAIL), :], tail_sem
        )
        tails.start()

        def finish(g, _):
            @pl.when(keys_s[0, g] >= 0)
            def _():
                for copy in copies(g):
                    copy.wait()

            return 0

        lax.fori_loop(0, groups, finish, 0)
        tails.wait()


def send_blocks(lists, images, precision, residual):
    groups, entries = lists.shape
    members = images.shape[1]
    nb_dev = images.shape[0] // BLK
    return pl.pallas_call(
        send_kernel,
        grid=(nb_dev // CHUNK,),
        in_specs=[
            pl.BlockSpec((groups, entries), lambda s: (0, 0)),
            pl.BlockSpec((CHUNK * BLK, members), lambda s: (s, 0)),
            pl.BlockSpec((CHUNK, BLK), lambda s: (s, 0)),
            pl.BlockSpec((CHUNK, BLK), lambda s: (s, 0)),
        ],
        out_specs=[
            pl.BlockSpec(memory_space=pl.ANY),
            pl.BlockSpec((8, entries), lambda s: (0, 0)),
        ],
        out_shape=[
            jax.ShapeDtypeStruct((groups, CAP * members + TAIL, BLK), jnp.bfloat16),
            jax.ShapeDtypeStruct((8, entries), jnp.int32),
        ],
        scratch_shapes=[
            pltpu.VMEM((nb_dev, members, BLK), jnp.bfloat16),
            pltpu.VMEM((nb_dev, BLK), jnp.float32),
            pltpu.VMEM((groups, TAIL, BLK), jnp.bfloat16),
            pltpu.VMEM((members, members), jnp.bfloat16),
            pltpu.VMEM((8, groups), jnp.int32),
            pltpu.SMEM((8, groups), jnp.int32),
            pltpu.SemaphoreType.DMA,
            pltpu.SemaphoreType.DMA,
            pltpu.SemaphoreType.DMA((CAP, groups)),
        ],
        compiler_params=pltpu.CompilerParams(vmem_limit_bytes=40 * 2**20),
        cost_estimate=pl.CostEstimate(
            flops=2 * images.shape[0] * members * members,
            bytes_accessed=24 * 2**20,
            transcendentals=0,
        ),
        name="send_blocks",
    )(lists, images, precision, residual)


def split(x):
    high = x.astype(jnp.bfloat16)
    return high, (x - high.astype(jnp.float32)).astype(jnp.bfloat16)


def dot3(a, b):
    ah, al = a
    bh, bl = b
    return dot(
        jnp.concatenate([ah, ah, al], axis=1), jnp.concatenate([bh, bl, bh], axis=0)
    )


def weights_kernel(table_ref, got_ref, out_ref, buf, yh, yl, zh, zl, sems):
    patches = out_ref.shape[0]
    members = out_ref.shape[1]
    entries = table_ref.shape[1]
    per_patch = entries // patches

    for q in range(patches):

        def fetch(e, _, q=q):
            slot = table_ref[0, q * per_patch + e]
            lane = pl.ds(pl.multiple_of(e * BLK, BLK), BLK)
            pltpu.make_async_copy(
                got_ref.at[slot // CAP, pl.ds(pl.multiple_of(slot % CAP * members, members), members), :],
                buf.at[q, pl.ds(0, members), lane],
                sems.at[q],
            ).start()
            pltpu.make_async_copy(
                got_ref.at[slot // CAP, pl.ds(CAP * members, TAIL), :],
                buf.at[q, pl.ds(members, TAIL), lane],
                sems.at[q],
            ).start()
            return 0

        lax.fori_loop(0, per_patch, fetch, 0)

    row, col = iotas((members, members))
    eye = jnp.where(row == col, 1.0, 0.0)
    norms = []
    ybars = []
    for q in range(patches):
        pltpu.make_async_copy(buf.at[q], buf.at[q], sems.at[q]).wait()
        for e in range(per_patch):
            lane = slice(e * BLK, (e + 1) * BLK)
            both = buf[q, members:, lane].astype(jnp.float32)
            second = table_ref[0, q * per_patch + e] % CAP == 1
            chosen = jnp.where(second, both[1:2, :], both[0:1, :])
            buf[q, members:, lane] = jnp.broadcast_to(chosen, (TAIL, BLK)).astype(jnp.bfloat16)
        both = dot(buf[q], buf[q, :members, :], NT)
        amat = (members - 1.0) * eye + both[:members]
        norm = jnp.sqrt(jnp.sum(amat * amat, keepdims=True) + 1e-06)
        norms.append(norm)
        ybars.append(both[members : members + 8])
        ysweep = amat / norm
        mid = split(1.5 * eye - 0.5 * ysweep)
        zh[q], zl[q] = mid
        yh[q], yl[q] = split(dot3(split(ysweep), mid))

    def middle(q):
        prod = dot3((zh[q], zl[q]), (yh[q], yl[q]))
        return split(1.5 * eye - 0.5 * prod)

    def sweep(_, carry):
        mids = [middle(q) for q in range(patches)]
        for q in range(patches):
            yh[q], yl[q] = split(dot3((yh[q], yl[q]), mids[q]))
            zh[q], zl[q] = split(dot3(mids[q], (zh[q], zl[q])))
        return carry

    lax.fori_loop(0, ITERS - 2, sweep, 0)
    for q in range(patches):
        root_inv = dot3(middle(q), (zh[q], zl[q])) / jnp.sqrt(norms[q])
        parts = split(root_inv)
        inner = dot3(split(ybars[q]), parts)
        mean_w = dot3(split(inner), parts)[0:1, :]
        out_ref[q] = (math.sqrt(members - 1.0) * root_inv + mean_w).astype(jnp.bfloat16)


def patch_weights(table, got, patches, members):
    entries = table.shape[1]
    per_patch = entries // patches
    square = pltpu.VMEM((patches, members, members), jnp.bfloat16)
    return pl.pallas_call(
        weights_kernel,
        in_specs=[
            pl.BlockSpec(memory_space=pltpu.SMEM),
            pl.BlockSpec(memory_space=pl.ANY),
        ],
        out_specs=pl.BlockSpec(memory_space=pltpu.VMEM),
        out_shape=jax.ShapeDtypeStruct((patches, members, members), jnp.bfloat16),
        scratch_shapes=[
            pltpu.VMEM((patches, members + TAIL, per_patch * BLK), jnp.bfloat16),
            square,
            square,
            square,
            square,
            pltpu.SemaphoreType.DMA((patches,)),
        ],
        compiler_params=pltpu.CompilerParams(vmem_limit_bytes=40 * 2**20),
        cost_estimate=pl.CostEstimate(
            flops=2 * patches * members * members * (entries // patches * BLK + 90 * members),
            bytes_accessed=64 * 2**20,
            transcendentals=0,
        ),
        name="patch_weights",
    )(table, got)


def analysis_kernel(tally_ref, w_ref, x_ref, out_ref):
    patches = pl.num_programs(0)
    block = lax.axis_index("patch") * lax.axis_size("mem") + lax.axis_index("mem")
    live = tally_ref[block * patches + pl.program_id(0)]
    prior = x_ref[...].astype(jnp.float32)
    mean = jnp.mean(prior, axis=0, keepdims=True)
    anomaly = (prior - mean).astype(jnp.bfloat16)
    blended = mean + dot(w_ref[0], anomaly)
    _, col = iotas((1, x_ref.shape[1]))
    out_ref[...] = jnp.where(col < live * NV, blended, prior).astype(jnp.bfloat16)


def analyse(tally, weights, state):
    patches, members, _ = weights.shape
    extent = state.shape[1] // patches
    return pl.pallas_call(
        analysis_kernel,
        grid=(patches,),
        in_specs=[
            pl.BlockSpec(memory_space=pltpu.SMEM),
            pl.BlockSpec((1, members, members), lambda q: (q, 0, 0)),
            pl.BlockSpec((members, extent), lambda q: (0, q)),
        ],
        out_specs=pl.BlockSpec((members, extent), lambda q: (0, q)),
        out_shape=jax.ShapeDtypeStruct(state.shape, jnp.bfloat16),
        compiler_params=pltpu.CompilerParams(vmem_limit_bytes=32 * 2**20),
        cost_estimate=pl.CostEstimate(
            flops=2 * members * members * state.shape[1],
            bytes_accessed=4 * members * state.shape[1],
            transcendentals=0,
        ),
        name="analysis",
    )(tally, weights, state)


def body(
    prior_states,
    member_obs_images,
    obs_residual,
    obs_precision_weights,
    region_obs_groups,
    active_profile_tally,
):
    devices = lax.axis_size("mem") * lax.axis_size("patch")
    members = member_obs_images.shape[1]
    patches = region_obs_groups.shape[0] // devices
    lists = region_obs_groups.reshape(devices, -1)
    send, table = send_blocks(
        lists,
        member_obs_images,
        obs_precision_weights.reshape(-1, BLK),
        obs_residual.reshape(-1, BLK),
    )
    got = lax.all_to_all(send, ("mem", "patch"), split_axis=0, concat_axis=0, tiled=True)
    got, prior_states = lax.optimization_barrier((got, prior_states))
    state = lax.all_to_all(prior_states, "mem", split_axis=1, concat_axis=0, tiled=True)
    weights = patch_weights(table, got, patches, members)
    result = analyse(active_profile_tally, weights, state)
    return lax.all_to_all(result, "mem", split_axis=0, concat_axis=1, tiled=True)


def solution(mesh):
    return jax.shard_map(
        body,
        mesh=mesh,
        in_specs=(
            P("mem", "patch"),
            P(("mem", "patch"), None),
            P(("mem", "patch")),
            P(("mem", "patch")),
            P(),
            P(),
        ),
        out_specs=P("mem", "patch"),
        check_vma=False,
    )
```

```python
import math

import jax
import jax.numpy as jnp
from jax import lax
from jax.experimental import pallas as pl
from jax.experimental.pallas import tpu as pltpu
from jax.sharding import PartitionSpec as P

NV = 128
BLK = 128
CAP = 2
ITERS = 10
TAIL = 16
CHUNK = 32
BIG = 1 << 30
LIVE = 4

NT = (((1,), (1,)), ((), ()))
NN = (((1,), (0,)), ((), ()))


def dot(a, b, dims=NN):
    return lax.dot_general(a, b, dims, preferred_element_type=jnp.float32)


def iotas(shape):
    return lax.broadcasted_iota(jnp.int32, shape, 0), lax.broadcasted_iota(jnp.int32, shape, 1)


def send_kernel(
    lists_ref, tally_ref, img_ref, prec_ref, resid_ref, prior_ref, send_ref, table_ref, fields_ref,
    img, prior, wt, innov, tail, square, keys, keys_s,
    img_sems, prior_sem, field_sems, key_sem, tail_sem, sems,
):
    nmem = lax.axis_size("mem")
    npat = lax.axis_size("patch")
    groups = send_ref.shape[0]
    per_patch, patches = lists_ref.shape[0], lists_ref.shape[1] // groups
    members = img.shape[1]
    nb_dev = wt.shape[0]
    steps = nb_dev // CHUNK
    me_m = lax.axis_index("mem")
    me_p = lax.axis_index("patch")
    source = me_m * npat + me_p

    def load(step):
        rows = pl.ds(step * CHUNK * BLK, CHUNK * BLK)
        return pltpu.make_async_copy(img_ref.at[rows, :], img.at[rows, :], img_sems.at[step])

    def place(g):
        return g % nmem * npat + g // nmem

    def field(part):
        extent = fields_ref.shape[2]
        return pltpu.make_async_copy(
            prior.at[:, pl.ds(part * extent, extent)], fields_ref.at[part], field_sems.at[part]
        )

    for step in range(steps):
        load(step).start()
    pltpu.make_async_copy(prior_ref, prior, prior_sem).start()

    blocks = lists_ref[...]
    row, col = iotas(blocks.shape)
    local = blocks - source * nb_dev
    mine = (local >= 0) & (local < nb_dev)
    key = (col % patches * per_patch + row) * nb_dev + local
    first = jnp.min(jnp.where(mine, key, BIG), axis=0, keepdims=True)
    last = jnp.max(jnp.where(mine, key, -1), axis=0, keepdims=True)
    firsts = first = jnp.broadcast_to(first, (8, first.shape[1]))
    lasts = last = jnp.broadcast_to(last, first.shape)
    for q in range(1, patches):
        firsts = jnp.minimum(firsts, pltpu.roll(first, first.shape[1] - q, 1))
        lasts = jnp.maximum(lasts, pltpu.roll(last, last.shape[1] - q, 1))
    keys[0:1, :] = jnp.where(lasts >= 0, firsts % nb_dev, -1)[0:1, :]
    keys[1:2, :] = jnp.where(lasts >= 0, lasts % nb_dev, -1)[0:1, :]
    pltpu.make_async_copy(keys, keys_s, key_sem).start()

    root = jnp.sqrt(prec_ref[...])
    innov[...] = root * resid_ref[...]
    row, col = iotas((members, members))
    centre = (jnp.where(row == col, 1.0, 0.0) - 1.0 / members).astype(jnp.bfloat16)
    pltpu.make_async_copy(keys, keys_s, key_sem).wait()
    row, _ = iotas((TAIL, BLK))

    def fill(g, _):
        one = innov[pl.ds(jnp.maximum(keys_s[0, g * patches], 0), 1), :]
        two = innov[pl.ds(jnp.maximum(keys_s[1, g * patches], 0), 1), :]
        tail[place(g)] = jnp.where(row == 0, one, two).astype(jnp.bfloat16)
        return 0

    lax.fori_loop(0, groups, fill, 0, unroll=8)
    tails = pltpu.make_async_copy(
        tail, send_ref.at[:, pl.ds(CAP * members, TAIL), :], tail_sem
    )
    tails.start()

    for step in range(steps):
        load(step).wait()
        for j in range(step * CHUNK, (step + 1) * CHUNK, 2):
            centred = dot(centre, img[j * BLK : (j + 2) * BLK, :], NT)
            wt[j] = (centred[:, :BLK] * root[j : j + 1, :]).astype(jnp.bfloat16)
            wt[j + 1] = (centred[:, BLK:] * root[j + 1 : j + 2, :]).astype(jnp.bfloat16)

    pltpu.make_async_copy(prior_ref, prior, prior_sem).wait()
    for part in range(fields_ref.shape[0]):
        field(part).start()

    def start(g, _):
        @pl.when(keys_s[0, g * patches] >= 0)
        def _():
            for c in range(CAP):
                pltpu.make_async_copy(
                    wt.at[keys_s[c, g * patches]],
                    send_ref.at[place(g), pl.ds(c * members, members), :],
                    sems.at[g],
                ).start()

        return 0

    lax.fori_loop(0, groups, start, 0, unroll=4)

    my_column = (me_p * nmem + me_m) * patches
    _, col = iotas(blocks.shape)
    _, lane = iotas((per_patch, 128))
    spread = jnp.zeros((per_patch, 128), jnp.int32)
    for q in range(patches):
        held = jnp.where(col == my_column + q, blocks // nb_dev, 0)
        spread = jnp.where(lane == q, jnp.sum(held, axis=1, keepdims=True), spread)
    square[0:per_patch, :] = spread
    turned = square[...].T
    row, col = iotas((per_patch, per_patch))
    for q in range(patches):
        here = turned[q : q + 1, 0:per_patch]
        slot = jnp.zeros_like(here)
        for other in range(q + 1):
            same = spread[:, other : other + 1] == here
            if other == q:
                same = same & (row < col)
            slot = jnp.maximum(slot, jnp.max(jnp.where(same, 1, 0), axis=0, keepdims=True))
        table_ref[q : q + 1, 0:per_patch] = here * CAP + slot
        table_ref[LIVE + q : LIVE + q + 1, :] = jnp.full((1, 128), tally_ref[my_column + q])

    def finish(g, _):
        @pl.when(keys_s[0, g * patches] >= 0)
        def _():
            slots = send_ref.at[place(g), pl.ds(0, CAP * members), :]
            pltpu.make_async_copy(slots, slots, sems.at[g]).wait()

        return 0

    lax.fori_loop(0, groups, finish, 0, unroll=4)
    tails.wait()
    for part in range(fields_ref.shape[0]):
        field(part).wait()


def send_blocks(lists, tally, images, precision, residual, prior, groups, nmem):
    members = images.shape[1]
    nb_dev = images.shape[0] // BLK
    return pl.pallas_call(
        send_kernel,
        in_specs=[
            pl.BlockSpec(memory_space=pltpu.VMEM),
            pl.BlockSpec(memory_space=pltpu.SMEM),
            pl.BlockSpec(memory_space=pl.ANY),
            pl.BlockSpec(memory_space=pltpu.VMEM),
            pl.BlockSpec(memory_space=pltpu.VMEM),
            pl.BlockSpec(memory_space=pl.ANY),
        ],
        out_specs=[
            pl.BlockSpec(memory_space=pl.ANY),
            pl.BlockSpec(memory_space=pltpu.VMEM),
            pl.BlockSpec(memory_space=pl.ANY),
        ],
        out_shape=[
            jax.ShapeDtypeStruct((groups, CAP * members + TAIL, BLK), jnp.bfloat16),
            jax.ShapeDtypeStruct((8, 128), jnp.int32),
            jax.ShapeDtypeStruct(
                (nmem, prior.shape[0], prior.shape[1] // nmem), prior.dtype
            ),
        ],
        scratch_shapes=[
            pltpu.VMEM(images.shape, jnp.bfloat16),
            pltpu.VMEM(prior.shape, jnp.bfloat16),
            pltpu.VMEM((nb_dev, members, BLK), jnp.bfloat16),
            pltpu.VMEM((nb_dev, BLK), jnp.float32),
            pltpu.VMEM((groups, TAIL, BLK), jnp.bfloat16),
            pltpu.VMEM((128, 128), jnp.int32),
            pltpu.VMEM((8, lists.shape[1]), jnp.int32),
            pltpu.SMEM((8, lists.shape[1]), jnp.int32),
            pltpu.SemaphoreType.DMA((nb_dev // CHUNK,)),
            pltpu.SemaphoreType.DMA,
            pltpu.SemaphoreType.DMA((nmem,)),
            pltpu.SemaphoreType.DMA,
            pltpu.SemaphoreType.DMA,
            pltpu.SemaphoreType.DMA((groups,)),
        ],
        compiler_params=pltpu.CompilerParams(vmem_limit_bytes=60 * 2**20),
        cost_estimate=pl.CostEstimate(
            flops=2 * images.shape[0] * members * members,
            bytes_accessed=24 * 2**20,
            transcendentals=0,
        ),
        name="send_blocks",
    )(lists, tally, images, precision, residual, prior)


def split(x):
    high = x.astype(jnp.bfloat16)
    return high, (x - high.astype(jnp.float32)).astype(jnp.bfloat16)


def dot3(a, b):
    ah, al = a
    bh, bl = b
    return dot(
        jnp.concatenate([ah, ah, al], axis=1), jnp.concatenate([bh, bl, bh], axis=0)
    )


def weights_kernel(table_ref, got_ref, out_ref, buf, yh, yl, zh, zl, sems):
    patches = out_ref.shape[0]
    members = out_ref.shape[1]
    per_patch = buf.shape[2] // BLK

    for q in range(patches):

        def fetch(e, _, q=q):
            slot = table_ref[q, e]
            lane = pl.ds(pl.multiple_of(e * BLK, BLK), BLK)
            pltpu.make_async_copy(
                got_ref.at[slot // CAP, pl.ds(pl.multiple_of(slot % CAP * members, members), members), :],
                buf.at[q, pl.ds(0, members), lane],
                sems.at[q],
            ).start()
            pltpu.make_async_copy(
                got_ref.at[slot // CAP, pl.ds(CAP * members, TAIL), :],
                buf.at[q, pl.ds(members, TAIL), lane],
                sems.at[q],
            ).start()
            return 0

        lax.fori_loop(0, per_patch, fetch, 0)

    row, col = iotas((members, members))
    eye = jnp.where(row == col, 1.0, 0.0)
    norms = []
    ybars = []
    for q in range(patches):
        pltpu.make_async_copy(buf.at[q], buf.at[q], sems.at[q]).wait()
        for e in range(per_patch):
            lane = slice(e * BLK, (e + 1) * BLK)
            both = buf[q, members:, lane].astype(jnp.float32)
            second = table_ref[q, e] % CAP == 1
            chosen = jnp.where(second, both[1:2, :], both[0:1, :])
            buf[q, members:, lane] = jnp.broadcast_to(chosen, (TAIL, BLK)).astype(jnp.bfloat16)
        both = dot(buf[q], buf[q, :members, :], NT)
        amat = (members - 1.0) * eye + both[:members]
        norm = jnp.sqrt(jnp.sum(amat * amat, keepdims=True) + 1e-06)
        norms.append(norm)
        ybars.append(both[members : members + 8])
        ysweep = amat / norm
        mid = split(1.5 * eye - 0.5 * ysweep)
        zh[q], zl[q] = mid
        yh[q], yl[q] = split(dot3(split(ysweep), mid))

    def middle(q):
        prod = dot3((zh[q], zl[q]), (yh[q], yl[q]))
        return split(1.5 * eye - 0.5 * prod)

    def sweep(_, carry):
        mids = [middle(q) for q in range(patches)]
        for q in range(patches):
            yh[q], yl[q] = split(dot3((yh[q], yl[q]), mids[q]))
            zh[q], zl[q] = split(dot3(mids[q], (zh[q], zl[q])))
        return carry

    lax.fori_loop(0, ITERS - 2, sweep, 0)
    for q in range(patches):
        root_inv = dot3(middle(q), (zh[q], zl[q])) / jnp.sqrt(norms[q])
        parts = split(root_inv)
        inner = dot3(split(ybars[q]), parts)
        mean_w = dot3(split(inner), parts)[0:1, :]
        out_ref[q] = (math.sqrt(members - 1.0) * root_inv + mean_w).astype(jnp.bfloat16)


def patch_weights(table, got, patches, per_patch, members):
    square = pltpu.VMEM((patches, members, members), jnp.bfloat16)
    return pl.pallas_call(
        weights_kernel,
        in_specs=[
            pl.BlockSpec(memory_space=pltpu.SMEM),
            pl.BlockSpec(memory_space=pl.ANY),
        ],
        out_specs=pl.BlockSpec(memory_space=pltpu.VMEM),
        out_shape=jax.ShapeDtypeStruct((patches, members, members), jnp.bfloat16),
        scratch_shapes=[
            pltpu.VMEM((patches, members + TAIL, per_patch * BLK), jnp.bfloat16),
            square,
            square,
            square,
            square,
            pltpu.SemaphoreType.DMA((patches,)),
        ],
        compiler_params=pltpu.CompilerParams(vmem_limit_bytes=40 * 2**20),
        cost_estimate=pl.CostEstimate(
            flops=2 * patches * members * members * (per_patch * BLK + 90 * members),
            bytes_accessed=64 * 2**20,
            transcendentals=0,
        ),
        name="patch_weights",
    )(table, got)


def analysis_kernel(table_ref, w_ref, x_ref, out_ref):
    live = table_ref[LIVE + pl.program_id(0), 0]
    prior = x_ref[...].astype(jnp.float32)
    mean = jnp.mean(prior, axis=0, keepdims=True)
    anomaly = (prior - mean).astype(jnp.bfloat16)
    blended = mean + dot(w_ref[0], anomaly)
    _, col = iotas((1, x_ref.shape[1]))
    out_ref[...] = jnp.where(col < live * NV, blended, prior).astype(jnp.bfloat16)


def analyse(table, weights, state):
    patches, members, _ = weights.shape
    extent = state.shape[1] // patches
    return pl.pallas_call(
        analysis_kernel,
        grid=(patches,),
        in_specs=[
            pl.BlockSpec(memory_space=pltpu.SMEM),
            pl.BlockSpec((1, members, members), lambda q: (q, 0, 0)),
            pl.BlockSpec((members, extent), lambda q: (0, q)),
        ],
        out_specs=pl.BlockSpec((members, extent), lambda q: (0, q)),
        out_shape=jax.ShapeDtypeStruct(state.shape, jnp.bfloat16),
        compiler_params=pltpu.CompilerParams(vmem_limit_bytes=32 * 2**20),
        cost_estimate=pl.CostEstimate(
            flops=2 * members * members * state.shape[1],
            bytes_accessed=4 * members * state.shape[1],
            transcendentals=0,
        ),
        name="analysis",
    )(table, weights, state)


def body(
    prior_states,
    member_obs_images,
    obs_residual,
    obs_precision_weights,
    region_obs_groups,
    active_profile_tally,
):
    devices = lax.axis_size("mem") * lax.axis_size("patch")
    members = member_obs_images.shape[1]
    patches = region_obs_groups.shape[0] // devices
    nmem = lax.axis_size("mem")
    send, table, fields = send_blocks(
        region_obs_groups.T,
        active_profile_tally,
        member_obs_images,
        obs_precision_weights.reshape(-1, BLK),
        obs_residual.reshape(-1, BLK),
        prior_states,
        devices,
        nmem,
    )
    got = lax.all_to_all(send, ("mem", "patch"), split_axis=0, concat_axis=0, tiled=True)
    got, fields = lax.optimization_barrier((got, fields))
    fields = lax.all_to_all(fields, "mem", split_axis=0, concat_axis=0, tiled=True)
    state = fields.reshape(members, -1)
    weights = patch_weights(table, got, patches, region_obs_groups.shape[1], members)
    result = analyse(table, weights, state)
    return lax.all_to_all(result, "mem", split_axis=0, concat_axis=1, tiled=True)


def solution(mesh):
    return jax.shard_map(
        body,
        mesh=mesh,
        in_specs=(
            P("mem", "patch"),
            P(("mem", "patch"), None),
            P(("mem", "patch")),
            P(("mem", "patch")),
            P(),
            P(),
        ),
        out_specs=P("mem", "patch"),
        check_vma=False,
    )
```

```python
import math

import jax
import jax.numpy as jnp
from jax import lax
from jax.experimental import pallas as pl
from jax.experimental.pallas import tpu as pltpu
from jax.sharding import PartitionSpec as P

NV = 128
BLK = 128
CAP = 2
ITERS = 10
TAIL = 16
CHUNK = 32
BIG = 1 << 30
LIVE = 4
RUN = 32

NT = (((1,), (1,)), ((), ()))
NN = (((1,), (0,)), ((), ()))


def dot(a, b, dims=NN):
    return lax.dot_general(a, b, dims, preferred_element_type=jnp.float32)


def iotas(shape):
    return lax.broadcasted_iota(jnp.int32, shape, 0), lax.broadcasted_iota(jnp.int32, shape, 1)


def send_kernel(
    lists_ref, tally_ref, img_ref, prec_ref, resid_ref, prior_ref, send_ref, table_ref, fields_ref,
    img, prior, wt, innov, tail, square, keys, keys_s,
    img_sems, prior_sem, field_sems, key_sem, tail_sem, sems,
):
    nmem = lax.axis_size("mem")
    npat = lax.axis_size("patch")
    groups = send_ref.shape[0]
    per_patch, patches = lists_ref.shape[0], lists_ref.shape[1] // groups
    members = img.shape[1]
    nb_dev = wt.shape[0]
    steps = nb_dev // CHUNK
    me_m = lax.axis_index("mem")
    me_p = lax.axis_index("patch")
    source = me_m * npat + me_p

    def load(step):
        rows = pl.ds(step * CHUNK * BLK, CHUNK * BLK)
        return pltpu.make_async_copy(img_ref.at[rows, :], img.at[rows, :], img_sems.at[step])

    def each(act):
        def column(p, _):
            for m in range(nmem):
                act(p * nmem + m, m * npat + p)
            return 0

        lax.fori_loop(0, npat, column, 0, unroll=2)

    def field(part):
        extent = fields_ref.shape[2]
        return pltpu.make_async_copy(
            prior.at[:, pl.ds(part * extent, extent)], fields_ref.at[part], field_sems.at[part]
        )

    for step in range(steps):
        load(step).start()
    pltpu.make_async_copy(prior_ref, prior, prior_sem).start()

    blocks = lists_ref[...]
    row, col = iotas(blocks.shape)
    local = blocks - source * nb_dev
    mine = (local >= 0) & (local < nb_dev)
    key = (col % patches * per_patch + row) * nb_dev + local
    first = jnp.min(jnp.where(mine, key, BIG), axis=0, keepdims=True)
    last = jnp.max(jnp.where(mine, key, -1), axis=0, keepdims=True)
    firsts = first = jnp.broadcast_to(first, (8, first.shape[1]))
    lasts = last = jnp.broadcast_to(last, first.shape)
    for q in range(1, patches):
        firsts = jnp.minimum(firsts, pltpu.roll(first, first.shape[1] - q, 1))
        lasts = jnp.maximum(lasts, pltpu.roll(last, last.shape[1] - q, 1))
    keys[0:1, :] = jnp.where(lasts >= 0, firsts % nb_dev, -1)[0:1, :]
    keys[1:2, :] = jnp.where(lasts >= 0, lasts % nb_dev, -1)[0:1, :]
    pltpu.make_async_copy(keys, keys_s, key_sem).start()

    root = jnp.sqrt(prec_ref[...])
    innov[...] = root * resid_ref[...]
    row, col = iotas((members, members))
    centre = (jnp.where(row == col, 1.0, 0.0) - 1.0 / members).astype(jnp.bfloat16)
    pltpu.make_async_copy(keys, keys_s, key_sem).wait()
    row, _ = iotas((TAIL, BLK))

    def fill(g, dest):
        one = innov[pl.ds(jnp.maximum(keys_s[0, g * patches], 0), 1), :]
        two = innov[pl.ds(jnp.maximum(keys_s[1, g * patches], 0), 1), :]
        tail[dest] = jnp.where(row == 0, one, two).astype(jnp.bfloat16)

    each(fill)
    tails = pltpu.make_async_copy(
        tail, send_ref.at[:, pl.ds(CAP * members, TAIL), :], tail_sem
    )
    tails.start()

    for step in range(steps):
        load(step).wait()
        for j in range(step * CHUNK, (step + 1) * CHUNK, 2):
            centred = dot(centre, img[j * BLK : (j + 2) * BLK, :], NT)
            wt[j] = (centred[:, :BLK] * root[j : j + 1, :]).astype(jnp.bfloat16)
            wt[j + 1] = (centred[:, BLK:] * root[j + 1 : j + 2, :]).astype(jnp.bfloat16)

    pltpu.make_async_copy(prior_ref, prior, prior_sem).wait()
    for part in range(fields_ref.shape[0]):
        field(part).start()

    def start(g, dest):
        @pl.when(keys_s[0, g * patches] >= 0)
        def _():
            for c in range(CAP):
                pltpu.make_async_copy(
                    wt.at[keys_s[c, g * patches]],
                    send_ref.at[dest, pl.ds(c * members, members), :],
                    sems.at[g],
                ).start()

    each(start)

    my_column = (me_p * nmem + me_m) * patches
    _, col = iotas(blocks.shape)
    _, lane = iotas((per_patch, 128))
    spread = jnp.zeros((per_patch, 128), jnp.int32)
    for q in range(patches):
        held = jnp.where(col == my_column + q, blocks // nb_dev, 0)
        spread = jnp.where(lane == q, jnp.sum(held, axis=1, keepdims=True), spread)
    square[0:per_patch, :] = spread
    turned = square[...].T
    row, col = iotas((per_patch, per_patch))
    for q in range(patches):
        here = turned[q : q + 1, 0:per_patch]
        slot = jnp.zeros_like(here)
        for other in range(q + 1):
            same = spread[:, other : other + 1] == here
            if other == q:
                same = same & (row < col)
            slot = jnp.maximum(slot, jnp.max(jnp.where(same, 1, 0), axis=0, keepdims=True))
        table_ref[q : q + 1, 0:per_patch] = here * CAP + slot
        table_ref[LIVE + q : LIVE + q + 1, :] = jnp.full((1, 128), tally_ref[my_column + q])

    def finish(g, dest):
        @pl.when(keys_s[0, g * patches] >= 0)
        def _():
            slots = send_ref.at[dest, pl.ds(0, CAP * members), :]
            pltpu.make_async_copy(slots, slots, sems.at[g]).wait()

    each(finish)
    tails.wait()
    for part in range(fields_ref.shape[0]):
        field(part).wait()


def send_blocks(lists, tally, images, precision, residual, prior, groups, nmem):
    members = images.shape[1]
    nb_dev = images.shape[0] // BLK
    return pl.pallas_call(
        send_kernel,
        in_specs=[
            pl.BlockSpec(memory_space=pltpu.VMEM),
            pl.BlockSpec(memory_space=pltpu.SMEM),
            pl.BlockSpec(memory_space=pl.ANY),
            pl.BlockSpec(memory_space=pltpu.VMEM),
            pl.BlockSpec(memory_space=pltpu.VMEM),
            pl.BlockSpec(memory_space=pl.ANY),
        ],
        out_specs=[
            pl.BlockSpec(memory_space=pl.ANY),
            pl.BlockSpec(memory_space=pltpu.VMEM),
            pl.BlockSpec(memory_space=pl.ANY),
        ],
        out_shape=[
            jax.ShapeDtypeStruct((groups, CAP * members + TAIL, BLK), jnp.bfloat16),
            jax.ShapeDtypeStruct((8, 128), jnp.int32),
            jax.ShapeDtypeStruct(
                (nmem, prior.shape[0], prior.shape[1] // nmem), prior.dtype
            ),
        ],
        scratch_shapes=[
            pltpu.VMEM(images.shape, jnp.bfloat16),
            pltpu.VMEM(prior.shape, jnp.bfloat16),
            pltpu.VMEM((nb_dev, members, BLK), jnp.bfloat16),
            pltpu.VMEM((nb_dev, BLK), jnp.float32),
            pltpu.VMEM((groups, TAIL, BLK), jnp.bfloat16),
            pltpu.VMEM((128, 128), jnp.int32),
            pltpu.VMEM((8, lists.shape[1]), jnp.int32),
            pltpu.SMEM((8, lists.shape[1]), jnp.int32),
            pltpu.SemaphoreType.DMA((nb_dev // CHUNK,)),
            pltpu.SemaphoreType.DMA,
            pltpu.SemaphoreType.DMA((nmem,)),
            pltpu.SemaphoreType.DMA,
            pltpu.SemaphoreType.DMA,
            pltpu.SemaphoreType.DMA((groups,)),
        ],
        compiler_params=pltpu.CompilerParams(vmem_limit_bytes=60 * 2**20),
        cost_estimate=pl.CostEstimate(
            flops=2 * images.shape[0] * members * members,
            bytes_accessed=24 * 2**20,
            transcendentals=0,
        ),
        name="send_blocks",
    )(lists, tally, images, precision, residual, prior)


def split(x):
    high = x.astype(jnp.bfloat16)
    return high, (x - high.astype(jnp.float32)).astype(jnp.bfloat16)


def dot3(a, b):
    ah, al = a
    bh, bl = b
    return dot(
        jnp.concatenate([ah, ah, al], axis=1), jnp.concatenate([bh, bl, bh], axis=0)
    )


def weights_kernel(table_ref, got_ref, out_ref, buf, tails, yh, yl, zh, zl, tail_sem, sems):
    patches = out_ref.shape[0]
    members = out_ref.shape[1]
    per_patch = buf.shape[1]

    tailing = pltpu.make_async_copy(
        got_ref.at[:, pl.ds(CAP * members, TAIL), :], tails, tail_sem
    )
    tailing.start()
    for q in range(patches):

        def fetch(e, _, q=q):
            slot = table_ref[q, e]
            first = pl.multiple_of(jnp.bitwise_and(slot, CAP - 1) * members, members)
            pltpu.make_async_copy(
                got_ref.at[lax.shift_right_logical(slot, 1), pl.ds(first, members), :],
                buf.at[q, e],
                sems.at[q],
            ).start()
            return 0

        lax.fori_loop(0, per_patch, fetch, 0, unroll=8)
    tailing.wait()

    row, col = iotas((members, members))
    eye = jnp.where(row == col, 1.0, 0.0)
    norms = []
    ybars = []
    for q in range(patches):
        both = jnp.zeros((members + TAIL, members), jnp.float32)
        scaled = []
        for e in range(per_patch):
            slot = table_ref[q, e]
            pair = tails[lax.shift_right_logical(slot, 1)].astype(jnp.float32)
            chosen = jnp.where(jnp.bitwise_and(slot, 1) == 1, pair[1:2, :], pair[0:1, :])
            scaled.append(jnp.broadcast_to(chosen, (TAIL, BLK)).astype(jnp.bfloat16))
        pltpu.make_async_copy(buf.at[q], buf.at[q], sems.at[q]).wait()
        for lo in range(0, per_patch, RUN):
            run = range(lo, min(lo + RUN, per_patch))
            rows = jnp.concatenate([buf[q, e] for e in run], axis=1)
            extra = jnp.concatenate([scaled[e] for e in run], axis=1)
            both = both + dot(jnp.concatenate([rows, extra], axis=0), rows, NT)
        amat = (members - 1.0) * eye + both[:members]
        norm = jnp.sqrt(jnp.sum(amat * amat, keepdims=True) + 1e-06)
        norms.append(norm)
        ybars.append(both[members : members + 8])
        ysweep = amat / norm
        mid = split(1.5 * eye - 0.5 * ysweep)
        zh[q], zl[q] = mid
        yh[q], yl[q] = split(dot3(split(ysweep), mid))

    def middle(q):
        prod = dot3((zh[q], zl[q]), (yh[q], yl[q]))
        return split(1.5 * eye - 0.5 * prod)

    def sweep(_, carry):
        mids = [middle(q) for q in range(patches)]
        for q in range(patches):
            yh[q], yl[q] = split(dot3((yh[q], yl[q]), mids[q]))
            zh[q], zl[q] = split(dot3(mids[q], (zh[q], zl[q])))
        return carry

    lax.fori_loop(0, ITERS - 2, sweep, 0, unroll=2)
    for q in range(patches):
        root_inv = dot3(middle(q), (zh[q], zl[q])) / jnp.sqrt(norms[q])
        parts = split(root_inv)
        inner = dot3(split(ybars[q]), parts)
        mean_w = dot3(split(inner), parts)[0:1, :]
        out_ref[q] = (math.sqrt(members - 1.0) * root_inv + mean_w).astype(jnp.bfloat16)


def patch_weights(table, got, patches, per_patch, members):
    square = pltpu.VMEM((patches, members, members), jnp.bfloat16)
    return pl.pallas_call(
        weights_kernel,
        in_specs=[
            pl.BlockSpec(memory_space=pltpu.SMEM),
            pl.BlockSpec(memory_space=pl.ANY),
        ],
        out_specs=pl.BlockSpec(memory_space=pltpu.VMEM),
        out_shape=jax.ShapeDtypeStruct((patches, members, members), jnp.bfloat16),
        scratch_shapes=[
            pltpu.VMEM((patches, per_patch, members, BLK), jnp.bfloat16),
            pltpu.VMEM((got.shape[0], TAIL, BLK), jnp.bfloat16),
            square,
            square,
            square,
            square,
            pltpu.SemaphoreType.DMA,
            pltpu.SemaphoreType.DMA((patches,)),
        ],
        compiler_params=pltpu.CompilerParams(vmem_limit_bytes=40 * 2**20),
        cost_estimate=pl.CostEstimate(
            flops=2 * patches * members * members * (per_patch * BLK + 90 * members),
            bytes_accessed=64 * 2**20,
            transcendentals=0,
        ),
        name="patch_weights",
    )(table, got)


def analysis_kernel(table_ref, w_ref, x_ref, out_ref):
    patches = w_ref.shape[0]
    extent = x_ref.shape[1] // patches
    _, col = iotas((1, extent))
    for q in range(patches):
        span = slice(q * extent, (q + 1) * extent)
        prior = x_ref[:, span].astype(jnp.float32)
        mean = jnp.mean(prior, axis=0, keepdims=True)
        anomaly = (prior - mean).astype(jnp.bfloat16)
        blended = mean + dot(w_ref[q], anomaly)
        live = col < table_ref[LIVE + q, 0] * NV
        out_ref[:, span] = jnp.where(live, blended, prior).astype(jnp.bfloat16)


def analyse(table, weights, state):
    patches, members, _ = weights.shape
    return pl.pallas_call(
        analysis_kernel,
        in_specs=[
            pl.BlockSpec(memory_space=pltpu.SMEM),
            pl.BlockSpec(memory_space=pltpu.VMEM),
            pl.BlockSpec(memory_space=pltpu.VMEM),
        ],
        out_specs=pl.BlockSpec(memory_space=pltpu.VMEM),
        out_shape=jax.ShapeDtypeStruct(state.shape, jnp.bfloat16),
        compiler_params=pltpu.CompilerParams(vmem_limit_bytes=32 * 2**20),
        cost_estimate=pl.CostEstimate(
            flops=2 * members * members * state.shape[1],
            bytes_accessed=4 * members * state.shape[1],
            transcendentals=0,
        ),
        name="analysis",
    )(table, weights, state)


def body(
    prior_states,
    member_obs_images,
    obs_residual,
    obs_precision_weights,
    region_obs_groups,
    active_profile_tally,
):
    devices = lax.axis_size("mem") * lax.axis_size("patch")
    members = member_obs_images.shape[1]
    patches = region_obs_groups.shape[0] // devices
    nmem = lax.axis_size("mem")
    send, table, fields = send_blocks(
        region_obs_groups.T,
        active_profile_tally,
        member_obs_images,
        obs_precision_weights.reshape(-1, BLK),
        obs_residual.reshape(-1, BLK),
        prior_states,
        devices,
        nmem,
    )
    got = lax.all_to_all(send, ("mem", "patch"), split_axis=0, concat_axis=0, tiled=True)
    got, fields = lax.optimization_barrier((got, fields))
    fields = lax.all_to_all(fields, "mem", split_axis=0, concat_axis=0, tiled=True)
    state = fields.reshape(members, -1)
    weights = patch_weights(table, got, patches, region_obs_groups.shape[1], members)
    result = analyse(table, weights, state)
    return lax.all_to_all(result, "mem", split_axis=0, concat_axis=1, tiled=True)


def solution(mesh):
    return jax.shard_map(
        body,
        mesh=mesh,
        in_specs=(
            P("mem", "patch"),
            P(("mem", "patch"), None),
            P(("mem", "patch")),
            P(("mem", "patch")),
            P(),
            P(),
        ),
        out_specs=P("mem", "patch"),
        check_vma=False,
    )
```

```python
import math

import jax
import jax.numpy as jnp
from jax import lax
from jax.experimental import pallas as pl
from jax.experimental.pallas import tpu as pltpu
from jax.sharding import PartitionSpec as P

NV = 128
BLK = 128
CAP = 2
ITERS = 10
TAIL = 8
CHUNK = 32
BIG = 1 << 30
LIVE = 4
RUN = 32
AHEAD = 4
EXTRA = 16

NT = (((1,), (1,)), ((), ()))
NN = (((1,), (0,)), ((), ()))


def dot(a, b, dims=NN):
    return lax.dot_general(a, b, dims, preferred_element_type=jnp.float32)


def iotas(shape):
    return lax.broadcasted_iota(jnp.int32, shape, 0), lax.broadcasted_iota(jnp.int32, shape, 1)


def send_kernel(
    lists_ref, tally_ref, img_ref, prec_ref, resid_ref, prior_ref, send_ref, table_ref, fields_ref,
    img, prior, wt, innov, tail, square, keys, keys_s,
    img_sems, prior_sem, field_sems, key_sem, tail_sem, sems,
):
    nmem = lax.axis_size("mem")
    npat = lax.axis_size("patch")
    groups = send_ref.shape[0]
    per_patch, patches = lists_ref.shape[0], lists_ref.shape[1] // groups
    members = img.shape[1]
    nb_dev = wt.shape[0]
    steps = nb_dev // CHUNK
    me_m = lax.axis_index("mem")
    me_p = lax.axis_index("patch")
    source = me_m * npat + me_p

    def load(step):
        rows = pl.ds(step * CHUNK * BLK, CHUNK * BLK)
        return pltpu.make_async_copy(img_ref.at[rows, :], img.at[rows, :], img_sems.at[step])

    def each(act):
        def column(p, _):
            for m in range(nmem):
                act(p * nmem + m, m * npat + p)
            return 0

        lax.fori_loop(0, npat, column, 0, unroll=2)

    def field(part):
        extent = fields_ref.shape[2]
        return pltpu.make_async_copy(
            prior.at[:, pl.ds(part * extent, extent)], fields_ref.at[part], field_sems.at[part]
        )

    for step in range(steps):
        load(step).start()
    pltpu.make_async_copy(prior_ref, prior, prior_sem).start()

    blocks = lists_ref[...]
    row, col = iotas(blocks.shape)
    local = blocks - source * nb_dev
    mine = (local >= 0) & (local < nb_dev)
    key = (col % patches * per_patch + row) * nb_dev + local
    first = jnp.min(jnp.where(mine, key, BIG), axis=0, keepdims=True)
    last = jnp.max(jnp.where(mine, key, -1), axis=0, keepdims=True)
    firsts = first = jnp.broadcast_to(first, (8, first.shape[1]))
    lasts = last = jnp.broadcast_to(last, first.shape)
    for q in range(1, patches):
        firsts = jnp.minimum(firsts, pltpu.roll(first, first.shape[1] - q, 1))
        lasts = jnp.maximum(lasts, pltpu.roll(last, last.shape[1] - q, 1))
    keys[0:1, :] = jnp.where(lasts >= 0, firsts % nb_dev, -1)[0:1, :]
    keys[1:2, :] = jnp.where(lasts >= 0, lasts % nb_dev, -1)[0:1, :]
    pltpu.make_async_copy(keys, keys_s, key_sem).start()

    root = jnp.sqrt(prec_ref[...])
    innov[...] = root * resid_ref[...]
    row, col = iotas((members, members))
    centre = (jnp.where(row == col, 1.0, 0.0) - 1.0 / members).astype(jnp.bfloat16)
    pltpu.make_async_copy(keys, keys_s, key_sem).wait()
    row, _ = iotas((TAIL, BLK))

    def fill(g, dest):
        one = innov[pl.ds(jnp.maximum(keys_s[0, g * patches], 0), 1), :]
        two = innov[pl.ds(jnp.maximum(keys_s[1, g * patches], 0), 1), :]
        tail[dest] = jnp.where(row == 0, one, two).astype(jnp.bfloat16)

    each(fill)
    tails = pltpu.make_async_copy(
        tail, send_ref.at[:, pl.ds(CAP * members, TAIL), :], tail_sem
    )
    tails.start()

    for step in range(steps):
        load(step).wait()
        for j in range(step * CHUNK, (step + 1) * CHUNK, 2):
            centred = dot(centre, img[j * BLK : (j + 2) * BLK, :], NT)
            wt[j] = (centred[:, :BLK] * root[j : j + 1, :]).astype(jnp.bfloat16)
            wt[j + 1] = (centred[:, BLK:] * root[j + 1 : j + 2, :]).astype(jnp.bfloat16)

    pltpu.make_async_copy(prior_ref, prior, prior_sem).wait()
    for part in range(fields_ref.shape[0]):
        field(part).start()

    def start(g, dest):
        @pl.when(keys_s[0, g * patches] >= 0)
        def _():
            for c in range(CAP):
                pltpu.make_async_copy(
                    wt.at[keys_s[c, g * patches]],
                    send_ref.at[dest, pl.ds(c * members, members), :],
                    sems.at[g],
                ).start()

    each(start)

    my_column = (me_p * nmem + me_m) * patches
    _, col = iotas(blocks.shape)
    _, lane = iotas((per_patch, 128))
    spread = jnp.zeros((per_patch, 128), jnp.int32)
    for q in range(patches):
        held = jnp.where(col == my_column + q, blocks // nb_dev, 0)
        spread = jnp.where(lane == q, jnp.sum(held, axis=1, keepdims=True), spread)
    square[0:per_patch, :] = spread
    turned = square[...].T
    row, col = iotas((per_patch, per_patch))
    for q in range(patches):
        here = turned[q : q + 1, 0:per_patch]
        slot = jnp.zeros_like(here)
        for other in range(q + 1):
            same = spread[:, other : other + 1] == here
            if other == q:
                same = same & (row < col)
            slot = jnp.maximum(slot, jnp.max(jnp.where(same, 1, 0), axis=0, keepdims=True))
        table_ref[q : q + 1, 0:per_patch] = here * CAP + slot
        table_ref[LIVE + q : LIVE + q + 1, :] = jnp.full((1, 128), tally_ref[my_column + q])

    def finish(g, dest):
        @pl.when(keys_s[0, g * patches] >= 0)
        def _():
            slots = send_ref.at[dest, pl.ds(0, CAP * members), :]
            pltpu.make_async_copy(slots, slots, sems.at[g]).wait()

    each(finish)
    tails.wait()
    for part in range(fields_ref.shape[0]):
        field(part).wait()


def send_blocks(lists, tally, images, precision, residual, prior, groups, nmem):
    members = images.shape[1]
    nb_dev = images.shape[0] // BLK
    return pl.pallas_call(
        send_kernel,
        in_specs=[
            pl.BlockSpec(memory_space=pltpu.VMEM),
            pl.BlockSpec(memory_space=pltpu.SMEM),
            pl.BlockSpec(memory_space=pl.ANY),
            pl.BlockSpec(memory_space=pltpu.VMEM),
            pl.BlockSpec(memory_space=pltpu.VMEM),
            pl.BlockSpec(memory_space=pl.ANY),
        ],
        out_specs=[
            pl.BlockSpec(memory_space=pl.ANY),
            pl.BlockSpec(memory_space=pltpu.VMEM),
            pl.BlockSpec(memory_space=pl.ANY),
        ],
        out_shape=[
            jax.ShapeDtypeStruct((groups, CAP * members + TAIL, BLK), jnp.bfloat16),
            jax.ShapeDtypeStruct((8, 128), jnp.int32),
            jax.ShapeDtypeStruct(
                (nmem, prior.shape[0], prior.shape[1] // nmem), prior.dtype
            ),
        ],
        scratch_shapes=[
            pltpu.VMEM(images.shape, jnp.bfloat16),
            pltpu.VMEM(prior.shape, jnp.bfloat16),
            pltpu.VMEM((nb_dev, members, BLK), jnp.bfloat16),
            pltpu.VMEM((nb_dev, BLK), jnp.float32),
            pltpu.VMEM((groups, TAIL, BLK), jnp.bfloat16),
            pltpu.VMEM((128, 128), jnp.int32),
            pltpu.VMEM((8, lists.shape[1]), jnp.int32),
            pltpu.SMEM((8, lists.shape[1]), jnp.int32),
            pltpu.SemaphoreType.DMA((nb_dev // CHUNK,)),
            pltpu.SemaphoreType.DMA,
            pltpu.SemaphoreType.DMA((nmem,)),
            pltpu.SemaphoreType.DMA,
            pltpu.SemaphoreType.DMA,
            pltpu.SemaphoreType.DMA((groups,)),
        ],
        compiler_params=pltpu.CompilerParams(vmem_limit_bytes=60 * 2**20),
        cost_estimate=pl.CostEstimate(
            flops=2 * images.shape[0] * members * members,
            bytes_accessed=24 * 2**20,
            transcendentals=0,
        ),
        name="send_blocks",
    )(lists, tally, images, precision, residual, prior)


def split(x):
    high = x.astype(jnp.bfloat16)
    return high, (x - high.astype(jnp.float32)).astype(jnp.bfloat16)


def dot3(a, b):
    ah, al = a
    bh, bl = b
    return dot(
        jnp.concatenate([ah, ah, al], axis=1), jnp.concatenate([bh, bl, bh], axis=0)
    )


def weights_kernel(table_ref, got_ref, out_ref, buf, tails, yh, yl, zh, zl, tail_sem, sems):
    patches = out_ref.shape[0]
    members = out_ref.shape[1]
    per_patch = buf.shape[1]

    tailing = pltpu.make_async_copy(
        got_ref.at[:, pl.ds(CAP * members, TAIL), :], tails, tail_sem
    )
    tailing.start()

    def gather(q):
        def fetch(e, _):
            slot = table_ref[q, e]
            first = pl.multiple_of(jnp.bitwise_and(slot, CAP - 1) * members, members)
            pltpu.make_async_copy(
                got_ref.at[lax.shift_right_logical(slot, 1), pl.ds(first, members), :],
                buf.at[q, e],
                sems.at[q],
            ).start()
            return 0

        lax.fori_loop(0, per_patch, fetch, 0, unroll=8)

    for q in range(min(AHEAD, patches)):
        gather(q)
    tailing.wait()

    row, col = iotas((members, members))
    eye = jnp.where(row == col, 1.0, 0.0)
    norms = []
    ybars = []
    for q in range(patches):
        both = jnp.zeros((members + EXTRA, members), jnp.float32)
        scaled = []
        for e in range(per_patch):
            slot = table_ref[q, e]
            pair = tails[lax.shift_right_logical(slot, 1)].astype(jnp.float32)
            chosen = jnp.where(jnp.bitwise_and(slot, 1) == 1, pair[1:2, :], pair[0:1, :])
            scaled.append(jnp.broadcast_to(chosen, (EXTRA, BLK)).astype(jnp.bfloat16))
        pltpu.make_async_copy(buf.at[q], buf.at[q], sems.at[q]).wait()
        if q + AHEAD < patches:
            gather(q + AHEAD)
        for lo in range(0, per_patch, RUN):
            run = range(lo, min(lo + RUN, per_patch))
            rows = jnp.concatenate([buf[q, e] for e in run], axis=1)
            extra = jnp.concatenate([scaled[e] for e in run], axis=1)
            both = both + dot(jnp.concatenate([rows, extra], axis=0), rows, NT)
        amat = (members - 1.0) * eye + both[:members]
        norm = jnp.sqrt(jnp.sum(amat * amat, keepdims=True) + 1e-06)
        norms.append(norm)
        ybars.append(both[members : members + 8])
        ysweep = amat / norm
        mid = split(1.5 * eye - 0.5 * ysweep)
        zh[q], zl[q] = mid
        yh[q], yl[q] = split(dot3(split(ysweep), mid))

    def middle(q):
        prod = dot3((zh[q], zl[q]), (yh[q], yl[q]))
        return split(1.5 * eye - 0.5 * prod)

    def sweep(_, carry):
        mids = [middle(q) for q in range(patches)]
        for q in range(patches):
            yh[q], yl[q] = split(dot3((yh[q], yl[q]), mids[q]))
            zh[q], zl[q] = split(dot3(mids[q], (zh[q], zl[q])))
        return carry

    lax.fori_loop(0, ITERS - 2, sweep, 0, unroll=2)
    for q in range(patches):
        root_inv = dot3(middle(q), (zh[q], zl[q])) / jnp.sqrt(norms[q])
        parts = split(root_inv)
        inner = dot3(split(ybars[q]), parts)
        mean_w = dot3(split(inner), parts)[0:1, :]
        out_ref[q] = (math.sqrt(members - 1.0) * root_inv + mean_w).astype(jnp.bfloat16)


def patch_weights(table, got, patches, per_patch, members):
    square = pltpu.VMEM((patches, members, members), jnp.bfloat16)
    return pl.pallas_call(
        weights_kernel,
        in_specs=[
            pl.BlockSpec(memory_space=pltpu.SMEM),
            pl.BlockSpec(memory_space=pl.ANY),
        ],
        out_specs=pl.BlockSpec(memory_space=pltpu.VMEM),
        out_shape=jax.ShapeDtypeStruct((patches, members, members), jnp.bfloat16),
        scratch_shapes=[
            pltpu.VMEM((patches, per_patch, members, BLK), jnp.bfloat16),
            pltpu.VMEM((got.shape[0], TAIL, BLK), jnp.bfloat16),
            square,
            square,
            square,
            square,
            pltpu.SemaphoreType.DMA,
            pltpu.SemaphoreType.DMA((patches,)),
        ],
        compiler_params=pltpu.CompilerParams(vmem_limit_bytes=40 * 2**20),
        cost_estimate=pl.CostEstimate(
            flops=2 * patches * members * members * (per_patch * BLK + 90 * members),
            bytes_accessed=64 * 2**20,
            transcendentals=0,
        ),
        name="patch_weights",
    )(table, got)


def analysis_kernel(table_ref, w_ref, x_ref, out_ref):
    patches = w_ref.shape[0]
    extent = x_ref.shape[1] // patches
    _, col = iotas((1, extent))
    for q in range(patches):
        span = slice(q * extent, (q + 1) * extent)
        prior = x_ref[:, span].astype(jnp.float32)
        mean = jnp.mean(prior, axis=0, keepdims=True)
        anomaly = (prior - mean).astype(jnp.bfloat16)
        blended = mean + dot(w_ref[q], anomaly)
        live = col < table_ref[LIVE + q, 0] * NV
        out_ref[:, span] = jnp.where(live, blended, prior).astype(jnp.bfloat16)


def analyse(table, weights, state):
    patches, members, _ = weights.shape
    return pl.pallas_call(
        analysis_kernel,
        in_specs=[
            pl.BlockSpec(memory_space=pltpu.SMEM),
            pl.BlockSpec(memory_space=pltpu.VMEM),
            pl.BlockSpec(memory_space=pltpu.VMEM),
        ],
        out_specs=pl.BlockSpec(memory_space=pltpu.VMEM),
        out_shape=jax.ShapeDtypeStruct(state.shape, jnp.bfloat16),
        compiler_params=pltpu.CompilerParams(vmem_limit_bytes=32 * 2**20),
        cost_estimate=pl.CostEstimate(
            flops=2 * members * members * state.shape[1],
            bytes_accessed=4 * members * state.shape[1],
            transcendentals=0,
        ),
        name="analysis",
    )(table, weights, state)


def body(
    prior_states,
    member_obs_images,
    obs_residual,
    obs_precision_weights,
    region_obs_groups,
    active_profile_tally,
):
    devices = lax.axis_size("mem") * lax.axis_size("patch")
    members = member_obs_images.shape[1]
    patches = region_obs_groups.shape[0] // devices
    nmem = lax.axis_size("mem")
    send, table, fields = send_blocks(
        region_obs_groups.T,
        active_profile_tally,
        member_obs_images,
        obs_precision_weights.reshape(-1, BLK),
        obs_residual.reshape(-1, BLK),
        prior_states,
        devices,
        nmem,
    )
    got = lax.all_to_all(send, ("mem", "patch"), split_axis=0, concat_axis=0, tiled=True)
    got, fields = lax.optimization_barrier((got, fields))
    fields = lax.all_to_all(fields, "mem", split_axis=0, concat_axis=0, tiled=True)
    state = fields.reshape(members, -1)
    weights = patch_weights(table, got, patches, region_obs_groups.shape[1], members)
    result = analyse(table, weights, state)
    return lax.all_to_all(result, "mem", split_axis=0, concat_axis=1, tiled=True)


def solution(mesh):
    return jax.shard_map(
        body,
        mesh=mesh,
        in_specs=(
            P("mem", "patch"),
            P(("mem", "patch"), None),
            P(("mem", "patch")),
            P(("mem", "patch")),
            P(),
            P(),
        ),
        out_specs=P("mem", "patch"),
        check_vma=False,
    )
```

```python
import math

import jax
import jax.numpy as jnp
from jax import lax
from jax.experimental import pallas as pl
from jax.experimental.pallas import tpu as pltpu
from jax.sharding import PartitionSpec as P

NV = 128
BLK = 128
CAP = 2
ITERS = 10
TAIL = 8
CHUNK = 32
BIG = 1 << 30
LIVE = 4
RUN = 32
AHEAD = 4
EXTRA = 16

NT = (((1,), (1,)), ((), ()))
NN = (((1,), (0,)), ((), ()))


def dot(a, b, dims=NN):
    return lax.dot_general(a, b, dims, preferred_element_type=jnp.float32)


def iotas(shape):
    return lax.broadcasted_iota(jnp.int32, shape, 0), lax.broadcasted_iota(jnp.int32, shape, 1)


def send_kernel(
    lists_ref, tally_ref, img_ref, prec_ref, resid_ref, prior_ref, send_ref, table_ref, fields_ref,
    img, prior, wt, innov, tail, square, keys, keys_s,
    img_sems, prior_sem, field_sems, key_sem, tail_sem, sems,
):
    nmem = lax.axis_size("mem")
    npat = lax.axis_size("patch")
    groups = send_ref.shape[0]
    per_patch, patches = lists_ref.shape[0], lists_ref.shape[1] // groups
    members = img.shape[1]
    nb_dev = wt.shape[0]
    steps = nb_dev // CHUNK
    me_m = lax.axis_index("mem")
    me_p = lax.axis_index("patch")
    source = me_m * npat + me_p

    def load(step):
        rows = pl.ds(step * CHUNK * BLK, CHUNK * BLK)
        return pltpu.make_async_copy(img_ref.at[rows, :], img.at[rows, :], img_sems.at[step])

    def each(act):
        def column(p, _):
            for m in range(nmem):
                act(p * nmem + m, m * npat + p)
            return 0

        lax.fori_loop(0, npat, column, 0, unroll=2)

    def field(part):
        extent = fields_ref.shape[2]
        return pltpu.make_async_copy(
            prior.at[:, pl.ds(part * extent, extent)], fields_ref.at[part], field_sems.at[part]
        )

    for step in range(steps):
        load(step).start()
    pltpu.make_async_copy(prior_ref, prior, prior_sem).start()

    blocks = lists_ref[...]
    row, col = iotas(blocks.shape)
    local = blocks - source * nb_dev
    mine = (local >= 0) & (local < nb_dev)
    key = (col % patches * per_patch + row) * nb_dev + local
    first = jnp.min(jnp.where(mine, key, BIG), axis=0, keepdims=True)
    last = jnp.max(jnp.where(mine, key, -1), axis=0, keepdims=True)
    firsts = first = jnp.broadcast_to(first, (8, first.shape[1]))
    lasts = last = jnp.broadcast_to(last, first.shape)
    for q in range(1, patches):
        firsts = jnp.minimum(firsts, pltpu.roll(first, first.shape[1] - q, 1))
        lasts = jnp.maximum(lasts, pltpu.roll(last, last.shape[1] - q, 1))
    keys[0:1, :] = jnp.where(lasts >= 0, firsts % nb_dev, -1)[0:1, :]
    keys[1:2, :] = jnp.where(lasts >= 0, lasts % nb_dev, -1)[0:1, :]
    pltpu.make_async_copy(keys, keys_s, key_sem).start()

    root = jnp.sqrt(prec_ref[...])
    innov[...] = root * resid_ref[...]
    row, col = iotas((members, members))
    centre = (jnp.where(row == col, 1.0, 0.0) - 1.0 / members).astype(jnp.bfloat16)
    pltpu.make_async_copy(keys, keys_s, key_sem).wait()
    row, _ = iotas((TAIL, BLK))

    def fill(g, dest):
        one = innov[pl.ds(jnp.maximum(keys_s[0, g * patches], 0), 1), :]
        two = innov[pl.ds(jnp.maximum(keys_s[1, g * patches], 0), 1), :]
        tail[dest] = jnp.where(row == 0, one, two).astype(jnp.bfloat16)

    each(fill)
    tails = pltpu.make_async_copy(
        tail, send_ref.at[:, pl.ds(CAP * members, TAIL), :], tail_sem
    )
    tails.start()

    for step in range(steps):
        load(step).wait()
        for j in range(step * CHUNK, (step + 1) * CHUNK, 2):
            centred = dot(centre, img[j * BLK : (j + 2) * BLK, :], NT)
            wt[j] = (centred[:, :BLK] * root[j : j + 1, :]).astype(jnp.bfloat16)
            wt[j + 1] = (centred[:, BLK:] * root[j + 1 : j + 2, :]).astype(jnp.bfloat16)

    pltpu.make_async_copy(prior_ref, prior, prior_sem).wait()
    for part in range(fields_ref.shape[0]):
        field(part).start()

    def start(g, dest):
        @pl.when(keys_s[0, g * patches] >= 0)
        def _():
            for c in range(CAP):
                pltpu.make_async_copy(
                    wt.at[keys_s[c, g * patches]],
                    send_ref.at[dest, pl.ds(c * members, members), :],
                    sems.at[g],
                ).start()

    each(start)

    my_column = (me_p * nmem + me_m) * patches
    _, col = iotas(blocks.shape)
    _, lane = iotas((per_patch, 128))
    spread = jnp.zeros((per_patch, 128), jnp.int32)
    for q in range(patches):
        held = jnp.where(col == my_column + q, blocks // nb_dev, 0)
        spread = jnp.where(lane == q, jnp.sum(held, axis=1, keepdims=True), spread)
    square[0:per_patch, :] = spread
    turned = square[...].T
    row, col = iotas((per_patch, per_patch))
    for q in range(patches):
        here = turned[q : q + 1, 0:per_patch]
        slot = jnp.zeros_like(here)
        for other in range(q + 1):
            same = spread[:, other : other + 1] == here
            if other == q:
                same = same & (row < col)
            slot = jnp.maximum(slot, jnp.max(jnp.where(same, 1, 0), axis=0, keepdims=True))
        table_ref[q : q + 1, 0:per_patch] = here * CAP + slot
        table_ref[LIVE + q : LIVE + q + 1, :] = jnp.full((1, 128), tally_ref[my_column + q])

    def finish(g, dest):
        @pl.when(keys_s[0, g * patches] >= 0)
        def _():
            slots = send_ref.at[dest, pl.ds(0, CAP * members), :]
            pltpu.make_async_copy(slots, slots, sems.at[g]).wait()

    each(finish)
    tails.wait()
    for part in range(fields_ref.shape[0]):
        field(part).wait()


def send_blocks(lists, tally, images, precision, residual, prior, groups, nmem):
    members = images.shape[1]
    nb_dev = images.shape[0] // BLK
    return pl.pallas_call(
        send_kernel,
        in_specs=[
            pl.BlockSpec(memory_space=pltpu.VMEM),
            pl.BlockSpec(memory_space=pltpu.SMEM),
            pl.BlockSpec(memory_space=pl.ANY),
            pl.BlockSpec(memory_space=pltpu.VMEM),
            pl.BlockSpec(memory_space=pltpu.VMEM),
            pl.BlockSpec(memory_space=pl.ANY),
        ],
        out_specs=[
            pl.BlockSpec(memory_space=pl.ANY),
            pl.BlockSpec(memory_space=pltpu.VMEM),
            pl.BlockSpec(memory_space=pl.ANY),
        ],
        out_shape=[
            jax.ShapeDtypeStruct((groups, CAP * members + TAIL, BLK), jnp.bfloat16),
            jax.ShapeDtypeStruct((8, 128), jnp.int32),
            jax.ShapeDtypeStruct(
                (nmem, prior.shape[0], prior.shape[1] // nmem), prior.dtype
            ),
        ],
        scratch_shapes=[
            pltpu.VMEM(images.shape, jnp.bfloat16),
            pltpu.VMEM(prior.shape, jnp.bfloat16),
            pltpu.VMEM((nb_dev, members, BLK), jnp.bfloat16),
            pltpu.VMEM((nb_dev, BLK), jnp.float32),
            pltpu.VMEM((groups, TAIL, BLK), jnp.bfloat16),
            pltpu.VMEM((128, 128), jnp.int32),
            pltpu.VMEM((8, lists.shape[1]), jnp.int32),
            pltpu.SMEM((8, lists.shape[1]), jnp.int32),
            pltpu.SemaphoreType.DMA((nb_dev // CHUNK,)),
            pltpu.SemaphoreType.DMA,
            pltpu.SemaphoreType.DMA((nmem,)),
            pltpu.SemaphoreType.DMA,
            pltpu.SemaphoreType.DMA,
            pltpu.SemaphoreType.DMA((groups,)),
        ],
        compiler_params=pltpu.CompilerParams(vmem_limit_bytes=60 * 2**20),
        cost_estimate=pl.CostEstimate(
            flops=2 * images.shape[0] * members * members,
            bytes_accessed=24 * 2**20,
            transcendentals=0,
        ),
        name="send_blocks",
    )(lists, tally, images, precision, residual, prior)


def split(x):
    high = x.astype(jnp.bfloat16)
    return high, (x - high.astype(jnp.float32)).astype(jnp.bfloat16)


def dot3(a, b):
    ah, al = a
    bh, bl = b
    return dot(
        jnp.concatenate([ah, ah, al], axis=1), jnp.concatenate([bh, bl, bh], axis=0)
    )


def weights_kernel(table_ref, got_ref, out_ref, buf, tails, yh, yl, zh, zl, tail_sem, sems):
    patches = out_ref.shape[0]
    members = out_ref.shape[1]
    per_patch = buf.shape[1]

    tailing = pltpu.make_async_copy(
        got_ref.at[:, pl.ds(CAP * members, TAIL), :], tails, tail_sem
    )
    tailing.start()

    def gather(q):
        def fetch(e, _):
            slot = table_ref[q, e]
            first = pl.multiple_of(jnp.bitwise_and(slot, CAP - 1) * members, members)
            pltpu.make_async_copy(
                got_ref.at[lax.shift_right_logical(slot, 1), pl.ds(first, members), :],
                buf.at[q, e],
                sems.at[q],
            ).start()
            return 0

        lax.fori_loop(0, per_patch, fetch, 0, unroll=8)

    for q in range(min(AHEAD, patches)):
        gather(q)
    tailing.wait()

    row, col = iotas((members, members))
    eye = jnp.where(row == col, 1.0, 0.0)
    norms = []
    ybars = []
    for q in range(patches):
        both = jnp.zeros((members + EXTRA, members), jnp.float32)
        scaled = []
        for e in range(per_patch):
            slot = table_ref[q, e]
            pair = tails[lax.shift_right_logical(slot, 1)].astype(jnp.float32)
            chosen = jnp.where(jnp.bitwise_and(slot, 1) == 1, pair[1:2, :], pair[0:1, :])
            scaled.append(jnp.broadcast_to(chosen, (EXTRA, BLK)).astype(jnp.bfloat16))
        pltpu.make_async_copy(buf.at[q], buf.at[q], sems.at[q]).wait()
        if q + AHEAD < patches:
            gather(q + AHEAD)
        for lo in range(0, per_patch, RUN):
            run = range(lo, min(lo + RUN, per_patch))
            rows = jnp.concatenate([buf[q, e] for e in run], axis=1)
            extra = jnp.concatenate([scaled[e] for e in run], axis=1)
            both = both + dot(jnp.concatenate([rows, extra], axis=0), rows, NT)
        amat = (members - 1.0) * eye + both[:members]
        norm = jnp.sqrt(jnp.sum(amat * amat, keepdims=True) + 1e-06)
        norms.append(norm)
        ybars.append(both[members : members + 8])
        ysweep = amat / norm
        mid = split(1.5 * eye - 0.5 * ysweep)
        zh[q], zl[q] = mid
        yh[q], yl[q] = split(dot3(split(ysweep), mid))

    def middle(q):
        prod = dot3((zh[q], zl[q]), (yh[q], yl[q]))
        return split(1.5 * eye - 0.5 * prod)

    def sweep(_, carry):
        mids = [middle(q) for q in range(patches)]
        for q in range(patches):
            yh[q], yl[q] = split(dot3((yh[q], yl[q]), mids[q]))
            zh[q], zl[q] = split(dot3(mids[q], (zh[q], zl[q])))
        return carry

    lax.fori_loop(0, ITERS - 2, sweep, 0, unroll=2)
    for q in range(patches):
        root_inv = dot3(middle(q), (zh[q], zl[q])) / jnp.sqrt(norms[q])
        parts = split(root_inv)
        inner = dot3(split(ybars[q]), parts)
        mean_w = dot3(split(inner), parts)[0:1, :]
        out_ref[q] = (math.sqrt(members - 1.0) * root_inv + mean_w).astype(jnp.bfloat16)


def patch_weights(table, got, patches, per_patch, members):
    square = pltpu.VMEM((patches, members, members), jnp.bfloat16)
    return pl.pallas_call(
        weights_kernel,
        in_specs=[
            pl.BlockSpec(memory_space=pltpu.SMEM),
            pl.BlockSpec(memory_space=pl.ANY),
        ],
        out_specs=pl.BlockSpec(memory_space=pltpu.VMEM),
        out_shape=jax.ShapeDtypeStruct((patches, members, members), jnp.bfloat16),
        scratch_shapes=[
            pltpu.VMEM((patches, per_patch, members, BLK), jnp.bfloat16),
            pltpu.VMEM((got.shape[0], TAIL, BLK), jnp.bfloat16),
            square,
            square,
            square,
            square,
            pltpu.SemaphoreType.DMA,
            pltpu.SemaphoreType.DMA((patches,)),
        ],
        compiler_params=pltpu.CompilerParams(vmem_limit_bytes=40 * 2**20),
        cost_estimate=pl.CostEstimate(
            flops=2 * patches * members * members * (per_patch * BLK + 90 * members),
            bytes_accessed=64 * 2**20,
            transcendentals=0,
        ),
        name="patch_weights",
    )(table, got)


def analysis_kernel(table_ref, w_ref, x_ref, out_ref):
    patches = w_ref.shape[0]
    extent = x_ref.shape[1] // patches
    members = x_ref.shape[0]
    _, col = iotas((1, extent))
    average = jnp.full((EXTRA, members), 1.0 / members, jnp.bfloat16)
    for q in range(patches):
        span = slice(q * extent, (q + 1) * extent)
        prior = x_ref[:, span]
        both = dot(jnp.concatenate([w_ref[q], average], axis=0), prior)
        rest = 1.0 - jnp.sum(w_ref[q].astype(jnp.float32), axis=1, keepdims=True)
        blended = (both[:members] + rest * both[members : members + 1]).astype(jnp.bfloat16)
        live = col < table_ref[LIVE + q, 0] * NV
        out_ref[:, span] = jnp.where(live, blended, prior)


def analyse(table, weights, state):
    patches, members, _ = weights.shape
    return pl.pallas_call(
        analysis_kernel,
        in_specs=[
            pl.BlockSpec(memory_space=pltpu.SMEM),
            pl.BlockSpec(memory_space=pltpu.VMEM),
            pl.BlockSpec(memory_space=pltpu.VMEM),
        ],
        out_specs=pl.BlockSpec(memory_space=pltpu.VMEM),
        out_shape=jax.ShapeDtypeStruct(state.shape, jnp.bfloat16),
        compiler_params=pltpu.CompilerParams(vmem_limit_bytes=32 * 2**20),
        cost_estimate=pl.CostEstimate(
            flops=2 * members * members * state.shape[1],
            bytes_accessed=4 * members * state.shape[1],
            transcendentals=0,
        ),
        name="analysis",
    )(table, weights, state)


def body(
    prior_states,
    member_obs_images,
    obs_residual,
    obs_precision_weights,
    region_obs_groups,
    active_profile_tally,
):
    devices = lax.axis_size("mem") * lax.axis_size("patch")
    members = member_obs_images.shape[1]
    patches = region_obs_groups.shape[0] // devices
    nmem = lax.axis_size("mem")
    send, table, fields = send_blocks(
        region_obs_groups.T,
        active_profile_tally,
        member_obs_images,
        obs_precision_weights.reshape(-1, BLK),
        obs_residual.reshape(-1, BLK),
        prior_states,
        devices,
        nmem,
    )
    got = lax.all_to_all(send, ("mem", "patch"), split_axis=0, concat_axis=0, tiled=True)
    got, fields = lax.optimization_barrier((got, fields))
    fields = lax.all_to_all(fields, "mem", split_axis=0, concat_axis=0, tiled=True)
    state = fields.reshape(members, -1)
    weights = patch_weights(table, got, patches, region_obs_groups.shape[1], members)
    result = analyse(table, weights, state)
    return lax.all_to_all(result, "mem", split_axis=0, concat_axis=1, tiled=True)


def solution(mesh):
    return jax.shard_map(
        body,
        mesh=mesh,
        in_specs=(
            P("mem", "patch"),
            P(("mem", "patch"), None),
            P(("mem", "patch")),
            P(("mem", "patch")),
            P(),
            P(),
        ),
        out_specs=P("mem", "patch"),
        check_vma=False,
    )
```
